256 devices in a mesh: row: 16 (over x, z_lo, core), col: 16 (over y, z_hi).
Axes of the slice: x: 4, y: 4, z: 8 (z_hi: 4, z_lo: 2; z = z_hi * 2 + z_lo), core: 2. Of those that a mesh axis runs over, the one named last changes fastest.
Arguments:
- features: bfloat16 [262144, 256], P('col', 'row'), may hold values from -6 to 6
- adjacency: bfloat16 [16, 16, 192, 128, 128], P('row', 'col'), may hold values from -0.15625 to 0.15625
- tile_coords: int32 [16, 16, 192, 2], P('row', 'col'), may hold values from 0 to 127, as said below
- tile_counts: int32 [16, 16], P('row', 'col'), may hold values from 1 to 192, as said below
- weight: bfloat16 [256, 256], replicated, may hold values from -0.375 to 0.375
- bias_vector: float32 [256], replicated, may hold values from -3 to 3
Outputs:
- embedded: bfloat16 [262144, 256], P(('row', 'col'))
The draws below stay inside these ranges and needn't reach their ends.
Inputs may be any that keep to these rules, and one draw needn't show every extreme that they name: `tile_coords`: live slots of one block name distinct tiles; the first entry is a tile row below 128, the second a tile column below 128; slots past the count hold 0 in both entries. `tile_counts`: every diagonal block (row block index equal to column block index) is full.
All inputs are finite; a program needn't handle non-finite values.
Results may differ from the reference program's by a relative error of at most 0.015.
Values may be sent and summed in bfloat16 or wider, within the bound.
No kernel may reach another device: no remote copies, remote signals or barrier semaphores. Data moves between devices by JAX's collectives and lax.ppermute only.
A program may use at most 128 MiB of HBM per device.

```python
import jax
import jax.numpy as jnp
from jax import lax

FEAT = 256
TILE = 128
MAXT = 192
GROUP = 32
ROW_TILES = 128
COL_TILES = 128
NODES = 262144
N_ROW = 16
N_COL = 16


def shared_counts(key):
    row_ids = jnp.arange(N_ROW, dtype=jnp.int32)[:, None]
    col_ids = jnp.arange(N_COL, dtype=jnp.int32)[None, :]
    distance = jnp.minimum(jnp.abs(row_ids - col_ids), 3)
    extra = jax.random.randint(jax.random.fold_in(key, 100), (N_ROW, N_COL), 0, MAXT // 4 + 2)
    base_count = jnp.right_shift(jnp.full((N_ROW, N_COL), MAXT, jnp.int32), distance)
    value = jnp.minimum(base_count + extra, MAXT)
    value = jnp.where(distance == 0, MAXT, value)
    return jnp.maximum(value, 1).astype(jnp.int32)


def draw_tile_counts(key, part):
    return shared_counts(key)


def draw_tile_coords(key, part):
    live_count = shared_counts(key)
    key = jax.random.fold_in(key, 7)
    device_keys = jax.random.split(key, N_ROW * N_COL)

    def pick_slots(device_key):
        return jax.random.permutation(device_key, ROW_TILES * COL_TILES)[:MAXT]
    slots = jax.vmap(pick_slots)(device_keys).reshape(N_ROW, N_COL, MAXT).astype(jnp.int32)
    tile_row = slots // COL_TILES
    tile_col = slots % COL_TILES
    live_mask = jnp.arange(MAXT, dtype=jnp.int32)[None, None, :] < live_count[:, :, None]
    stacked = jnp.stack([jnp.where(live_mask, tile_row, 0), jnp.where(live_mask, tile_col, 0)], axis=-1)
    return stacked.astype(jnp.int32)


def steps_of(key, shape, cuts, least, largest):
    def one(position, blocks):
        heights = jax.random.uniform(jax.random.fold_in(jax.random.fold_in(key, 6), position), (blocks,), jnp.float32, least / len(cuts), largest / len(cuts))
        return jnp.repeat(jnp.exp(heights), shape[position] // blocks).reshape((-1,) + (1,) * (len(shape) - position - 1))

    loudness = one(*cuts[0])
    for cut in cuts[1:]:
        loudness = loudness * one(*cut)
    return loudness


def gaussian(own_key, extent, spread, reach, cuts=(), kind=jnp.bfloat16):
    drawn = spread * jax.random.normal(own_key, extent, jnp.float32)
    if cuts:
        drawn = drawn * steps_of(own_key, extent, cuts, -0.22, 0.18)
    return jnp.clip(drawn, -reach, reach).astype(kind)


def setup_inputs(seed: int = 0) -> dict:
    key_list = jax.random.split(jax.random.key(seed), 7)
    features = gaussian(key_list[0], (NODES, FEAT), 1.0, 6.0, ((0, 16), (1, 16)))
    adjacency = gaussian(key_list[1], (N_ROW, N_COL, MAXT, TILE, TILE), (TILE * 12) ** -0.5, 0.15625, ((0, 16), (1, 16)))
    tile_coords = draw_tile_coords(jax.random.fold_in(key_list[6], 71), 0)
    tile_counts = draw_tile_counts(jax.random.fold_in(key_list[6], 71), 0)
    weight = gaussian(key_list[4], (FEAT, FEAT), FEAT ** -0.5, 0.375)
    bias_vector = gaussian(key_list[5], (FEAT,), 0.5, 3.0, (), jnp.float32)
    return {"features": features, "adjacency": adjacency, "tile_coords": tile_coords, "tile_counts": tile_counts, "weight": weight, "bias_vector": bias_vector}


def device_sum(tile_block, place_block, live_count, source_tiles):
    def add_group(group_index, running):
        first_slot = (group_index * GROUP).astype(jnp.int32)
        tile_values = lax.dynamic_slice_in_dim(tile_block, first_slot, GROUP, 0).astype(jnp.float32)
        tile_place = lax.dynamic_slice_in_dim(place_block, first_slot, GROUP, 0)
        live_mask = (first_slot + jnp.arange(GROUP, dtype=jnp.int32)) < live_count
        source = jnp.take(source_tiles, tile_place[:, 1], axis=0).astype(jnp.float32)
        product = jnp.einsum("gmn,gnf->gmf", tile_values, source)
        product = jnp.where(live_mask[:, None, None], product, jnp.float32(0.0))
        return running.at[tile_place[:, 0]].add(product)

    running = jnp.zeros((ROW_TILES, TILE, FEAT), jnp.float32)
    return lax.fori_loop(0, MAXT // GROUP, add_group, running)


def reference(features, adjacency, tile_coords, tile_counts, weight, bias_vector):
    source_blocks = features.reshape(N_COL, COL_TILES, TILE, FEAT)

    def row_block(row_index):
        def add_column(running, column_index):
            term = device_sum(adjacency[row_index, column_index], tile_coords[row_index, column_index],
                              tile_counts[row_index, column_index], source_blocks[column_index])
            rounded = lax.optimization_barrier(term.astype(jnp.bfloat16))
            return running + rounded.astype(jnp.float32), None

        start = jnp.zeros((ROW_TILES, TILE, FEAT), jnp.float32)
        running, unused = lax.scan(add_column, start, jnp.arange(N_COL, dtype=jnp.int32))
        hidden = running.reshape(ROW_TILES * TILE, FEAT).astype(jnp.bfloat16)
        mixed_rows = jnp.dot(hidden, weight, preferred_element_type=jnp.float32) + bias_vector
        return jnp.maximum(mixed_rows, jnp.float32(0.0)).astype(jnp.bfloat16)

    stacked = lax.map(row_block, jnp.arange(N_ROW, dtype=jnp.int32))
    return stacked.reshape(NODES, FEAT)
```

```python
import functools
import jax
import jax.numpy as jnp
from jax import lax
from jax.experimental import pallas as pl
from jax.experimental.pallas import tpu as pltpu
from jax.sharding import PartitionSpec as P

UNROLL = 8
PIECES = 5
SLICE = 16
LOTS = 4
VMEM_LIMIT = 58 * 2**20
X, Y, Z = 4, 4, 4


def tile_kernel(place_ref, count_ref, order_ref, *refs):
    sources, outs = refs[:-PIECES - 4], refs[-PIECES - 4:-4]
    total, x_ref, a_ref, sems = refs[-4:]
    *x_sources, a_source = sources[:x_ref.shape[0] // SLICE + 1]
    rows = total.shape[0] - 1
    slots, side = a_ref.shape[0], a_ref.shape[-1]
    lot = slots // LOTS
    x_copies = [
        pltpu.make_async_copy(source, x_ref.at[pl.ds(k * SLICE, SLICE)], sems.at[k])
        for k, source in enumerate(x_sources)
    ]
    a_copies = [
        pltpu.make_async_copy(
            a_source.at[pl.ds(k * lot, lot)], a_ref.at[pl.ds(k * lot, lot)], sems.at[len(x_sources) + k]
        )
        for k in range(LOTS)
    ]
    for copy in x_copies + a_copies:
        copy.start()

    def clear(i, c):
        total[i] = jnp.zeros(total.shape[1:], jnp.float32)
        return c

    lax.fori_loop(0, rows, clear, 0, unroll=4)
    count = count_ref[0]

    def add_tiles(group, c):
        products = []
        for u in range(UNROLL):
            slot = group * UNROLL + u
            row = jnp.where(slot < count, place_ref[0, slot], rows)
            nodes = pl.ds(pl.multiple_of(place_ref[1, slot] * side, side), side)
            product = lax.dot_general(
                x_ref[:, nodes], a_ref[slot], (((1,), (1,)), ((), ())), preferred_element_type=jnp.float32
            )
            products.append((row, product))
        for row, product in products:
            total[row] += product
        return c

    for copy in x_copies:
        copy.wait()
    groups = lot // UNROLL
    for k in range(LOTS):
        a_copies[k].wait()
        last = jnp.minimum(pl.cdiv(count, UNROLL), (k + 1) * groups)
        lax.fori_loop(k * groups, last, add_tiles, 0)
    per = rows // (Y * Z)
    step = 0
    for out in outs:
        for place in range(out.shape[0] // per):
            start = order_ref[step] * per
            step += 1
            for i in range(per):
                out[place * per + i] = total[start + i].astype(jnp.bfloat16)


def partial_pieces(place, count, order, xs, tiles, rows, *before):
    feat, side = sum(x.shape[0] for x in xs), tiles.shape[-1]
    smem = pl.BlockSpec(memory_space=pltpu.SMEM)
    vmem = pl.BlockSpec(memory_space=pltpu.VMEM)
    hbm = pl.BlockSpec(memory_space=pltpu.HBM)
    piece = lambda part: jax.ShapeDtypeStruct((rows // part, feat, side), jnp.bfloat16)
    return pl.pallas_call(
        tile_kernel,
        out_shape=[piece(4), piece(4), piece(8), piece(8), piece(4)],
        in_specs=[smem, smem, smem] + [hbm] * (len(xs) + 1) + [pl.BlockSpec(memory_space=pl.ANY)] * len(before),
        out_specs=[vmem] * PIECES,
        scratch_shapes=[
            pltpu.VMEM((rows + 1, feat, side), jnp.float32),
            pltpu.VMEM((feat, xs[0].shape[1]), jnp.bfloat16),
            pltpu.VMEM(tiles.shape, jnp.bfloat16),
            pltpu.SemaphoreType.DMA((len(xs) + LOTS,)),
        ],
        compiler_params=pltpu.CompilerParams(vmem_limit_bytes=VMEM_LIMIT),
        name="tile_sum",
    )(place, count, order, *xs, tiles, *before)


def along_y(step):
    return [(y * Z + z, ((y + step) % Y) * Z + z) for y in range(Y) for z in range(Z)]


def along_z(step):
    return [(y * Z + z, y * Z + (z + step) % Z) for y in range(Y) for z in range(Z)]


def add(*terms):
    out = terms[0].astype(jnp.float32)
    for term in terms[1:]:
        out = out + term.astype(jnp.float32)
    return out.astype(jnp.bfloat16)


def send(v, perm):
    return lax.ppermute(v, "col", perm)


def start_y(pieces):
    return send(pieces[2], along_y(1)), send(pieces[3], along_y(-1))


def relay_y(pieces, far):
    next_up, next_down = pieces[1], pieces[4]
    half = pieces[2].shape[0]
    up = jnp.concatenate([add(next_up[:half], far[0]), next_up[half:]])
    down = jnp.concatenate([next_down[:half], add(next_down[half:], far[1])])
    return up, down


def end_y(pieces, up, down):
    near_up, near_down = send(up, along_y(1)), send(down, along_y(-1))
    own = pieces[0]
    n = own.shape[0] // Z
    return [add(*(t[d * n:(d + 1) * n] for t in (own, near_up, near_down))) for d in range(Z)]


def sum_z(mine):
    return add(mine[0], *(send(mine[d], along_z(d)) for d in (1, 2, 3)))


def row_step(along_x, other_z, other_core):
    return [
        (r, (((r >> 2) + along_x) % X) * 4 + ((r & 3) ^ (2 * other_z) ^ other_core)) for r in range(4 * X)
    ]


def then(first, values):
    return lax.optimization_barrier((first, values))[1]


def shards(features, adjacency, tile_coords, tile_counts, weight, bias_vector):
    tiles = adjacency[0, 0]
    rows = 8 * lax.axis_size("col")
    place = tile_coords[0, 0].T
    count = tile_counts[0]
    me = lax.axis_index("col")
    y, z = me // Z, me % Z
    order = jnp.stack([
        ((y + dy) % Y) * Z + (z + dz) % Z
        for dy, dzs in ((0, range(4)), (1, range(4)), (2, (0, 1)), (2, (2, 3)), (3, range(4)))
        for dz in dzs
    ])
    kernel = lambda xs, *before: partial_pieces(place, count, order, xs, tiles, rows, *before)
    own = features.T
    weights = weight.reshape(lax.axis_size("row"), own.shape[0], -1)
    r = lax.axis_index("row")

    def product(hidden, steps):
        source = jnp.stack([((r // 4 + dx) % X) * 4 + ((r % 4) ^ (2 * dz) ^ core) for dx, dz, core in steps])
        w = weights[source].reshape(hidden.shape[1], -1)
        return jnp.einsum("tfm,fg->tmg", hidden, w, preferred_element_type=jnp.float32)

    get = lambda v, *step: lax.ppermute(v, "row", row_step(*step))
    swap = lambda vs: [get(v, 0, 0, 1) for v in vs]
    pair = get(own, 0, 1, 0)
    side = [get(own, 1, 0, 0), get(own, -1, 0, 0)]
    near = [own, pair]
    near += swap(near)
    pieces_a = kernel(near, *side)
    side += [get(pair, 1, 0, 0), get(pair, -1, 0, 0)]
    far_a = start_y(pieces_a)
    side = then(pieces_a, side)
    swapped = swap(side)
    relay_a = relay_y(pieces_a, far_a)
    pieces_b = kernel(side + swapped, *relay_a)
    side = then(swapped, side)
    far = [get(side[0], 1, 0, 0), get(side[3], -1, 0, 0)]
    mine_a = end_y(pieces_a, *relay_a)
    far_b = start_y(pieces_b)
    far = then(pieces_b, far)
    pieces_c = kernel(far + swap(far), *mine_a)
    hidden_a = sum_z(mine_a)
    far_c = start_y(pieces_c)
    relay_b = relay_y(pieces_b, far_b)
    mine_b = end_y(pieces_b, *relay_b)
    relay_c = relay_y(pieces_c, then(hidden_a, far_c))
    mine_c = end_y(pieces_c, *relay_c)
    hidden_b = sum_z(mine_b)
    hidden_c = sum_z(mine_c)
    on = lambda chunk: [(dx, dz, core) for core in range(2) for dx, dz in chunk]
    mixed = bias_vector + product(hidden_a, on([(0, 0), (0, 1)]))
    mixed = mixed + product(hidden_b, on([(-1, 0), (1, 0), (-1, 1), (1, 1)]))
    mixed = mixed + product(hidden_c, on([(2, 0), (2, 1)]))
    embedded = jnp.maximum(mixed, jnp.float32(0.0)).astype(jnp.bfloat16)
    return embedded.reshape(-1, embedded.shape[-1])


def solution(mesh):
    in_specs = (
        P("col", "row"),
        P("row", "col", None, None, None),
        P("row", "col", None, None),
        P("row", "col"),
        P(),
        P(),
    )
    out_specs = P(("row", "col"), None)
    return jax.shard_map(shards, mesh=mesh, in_specs=in_specs, out_specs=out_specs, check_vma=False)
```

```python
import functools
import jax
import jax.numpy as jnp
from jax import lax
from jax.experimental import pallas as pl
from jax.experimental.pallas import tpu as pltpu
from jax.sharding import PartitionSpec as P

UNROLL = 8
WHOLE = (4, 4, 4, 4)
HALVED = (8,) * 8
SLICE = 16
LOTS = 4
VMEM_LIMIT = 46 * 2**20
X, Y, Z = 4, 4, 4


def tile_kernel(pieces, place_ref, count_ref, order_ref, *refs):
    sources, outs = refs[:-pieces - 4], refs[-pieces - 4:-4]
    total, x_ref, a_ref, sems = refs[-4:]
    *x_sources, a_source = sources[:x_ref.shape[0] // SLICE + 1]
    rows = total.shape[0] - 1
    slots, side = a_ref.shape[0], a_ref.shape[-1]
    lot = slots // LOTS
    x_copies = [
        pltpu.make_async_copy(source, x_ref.at[pl.ds(k * SLICE, SLICE)], sems.at[k])
        for k, source in enumerate(x_sources)
    ]
    a_copies = [
        pltpu.make_async_copy(
            a_source.at[pl.ds(k * lot, lot)], a_ref.at[pl.ds(k * lot, lot)], sems.at[len(x_sources) + k]
        )
        for k in range(LOTS)
    ]
    for copy in x_copies + a_copies:
        copy.start()

    def clear(i, c):
        total[i] = jnp.zeros(total.shape[1:], jnp.float32)
        return c

    lax.fori_loop(0, rows, clear, 0, unroll=4)
    count = count_ref[0]

    def add_tiles(group, c):
        products = []
        for u in range(UNROLL):
            slot = group * UNROLL + u
            row = jnp.where(slot < count, place_ref[0, slot], rows)
            nodes = pl.ds(pl.multiple_of(place_ref[1, slot] * side, side), side)
            product = lax.dot_general(
                x_ref[:, nodes], a_ref[slot], (((1,), (1,)), ((), ())), preferred_element_type=jnp.float32
            )
            products.append((row, product))
        for row, product in products:
            total[row] += product
        return c

    for copy in x_copies:
        copy.wait()
    groups = lot // UNROLL
    for k in range(LOTS):
        a_copies[k].wait()
        last = jnp.minimum(pl.cdiv(count, UNROLL), (k + 1) * groups)
        lax.fori_loop(k * groups, last, add_tiles, 0)
    per = rows // (Y * Z)
    step = 0
    for out in outs:
        for place in range(out.shape[0] // per):
            start = order_ref[step] * per
            step += 1
            for i in range(per):
                out[place * per + i] = total[start + i].astype(jnp.bfloat16)


def partial_pieces(place, count, order, xs, tiles, rows, parts, *before):
    feat, side = sum(x.shape[0] for x in xs), tiles.shape[-1]
    smem = pl.BlockSpec(memory_space=pltpu.SMEM)
    vmem = pl.BlockSpec(memory_space=pltpu.VMEM)
    hbm = pl.BlockSpec(memory_space=pltpu.HBM)
    piece = lambda part: jax.ShapeDtypeStruct((rows // part, feat, side), jnp.bfloat16)
    return pl.pallas_call(
        functools.partial(tile_kernel, len(parts)),
        out_shape=[piece(part) for part in parts],
        in_specs=[smem, smem, smem] + [hbm] * (len(xs) + 1) + [pl.BlockSpec(memory_space=pl.ANY)] * len(before),
        out_specs=[vmem] * len(parts),
        scratch_shapes=[
            pltpu.VMEM((rows + 1, feat, side), jnp.float32),
            pltpu.VMEM((feat, xs[0].shape[1]), jnp.bfloat16),
            pltpu.VMEM(tiles.shape, jnp.bfloat16),
            pltpu.SemaphoreType.DMA((len(xs) + LOTS,)),
        ],
        compiler_params=pltpu.CompilerParams(vmem_limit_bytes=VMEM_LIMIT),
        name="tile_sum",
    )(place, count, order, *xs, tiles, *before)


def along_y(step):
    return [(y * Z + z, ((y + step) % Y) * Z + z) for y in range(Y) for z in range(Z)]


def along_z(step):
    return [(y * Z + z, y * Z + (z + step) % Z) for y in range(Y) for z in range(Z)]


def add(*terms):
    out = terms[0].astype(jnp.float32)
    for term in terms[1:]:
        out = out + term.astype(jnp.float32)
    return out.astype(jnp.bfloat16)


def send(v, perm):
    return lax.ppermute(v, "col", perm)


def start_y(pieces):
    return send(pieces[4], along_y(1)), send(pieces[5], along_y(-1))


def plain_y(pieces):
    return send(pieces[3], along_y(1)), send(pieces[6], along_y(-1))


def relay_kernel(*refs):
    for near, far, out in zip(refs[:2], refs[2:4], refs[4:]):
        out[...] = (near[...].astype(jnp.float32) + far[...].astype(jnp.float32)).astype(jnp.bfloat16)


def relay_y(pieces, far):
    vmem = pl.BlockSpec(memory_space=pltpu.VMEM)
    out = jax.ShapeDtypeStruct(far[0].shape, far[0].dtype)
    return pl.pallas_call(
        relay_kernel,
        out_shape=[out, out],
        in_specs=[vmem] * 4,
        out_specs=[vmem] * 2,
        compiler_params=pltpu.CompilerParams(vmem_limit_bytes=8 * 2**20),
        name="relay_y",
    )(pieces[2], pieces[7], *far)


def relay_z(up, down, far_up, far_down):
    block = lambda index: pl.BlockSpec(far_up.shape, lambda i: (index, 0, 0))
    return pl.pallas_call(
        relay_kernel,
        grid=(1,),
        out_shape=[jax.ShapeDtypeStruct(up.shape, up.dtype)] * 2,
        in_specs=[block(0), block(1), block(0), block(0)],
        out_specs=[block(0), block(1)],
        input_output_aliases={0: 0, 1: 1},
        compiler_params=pltpu.CompilerParams(vmem_limit_bytes=8 * 2**20),
        name="relay_z",
    )(up, down, far_up, far_down)


def sum_kernel(wholes, *refs):
    whole, halved, outs = refs[:wholes], refs[wholes:-5], refs[-5:]
    mine_ref, up_ref, far_up_ref, far_down_ref, down_ref = outs
    n = mine_ref.shape[0]

    def total(refs, tile):
        out = refs[0][tile].astype(jnp.float32)
        for ref in refs[1:]:
            out = out + ref[tile].astype(jnp.float32)
        return out.astype(jnp.bfloat16)

    def put(out_ref, tile, d, i):
        few = whole[0].shape[1]
        out_ref[tile, :few] = total(whole, d * n + i)
        if halved:
            out_ref[tile, few:] = total(halved[:3] if d < 2 else halved[3:], (d % 2) * n + i)

    for i in range(n):
        put(mine_ref, i, 0, i)
        put(up_ref, i, 1, i)
        put(far_up_ref if i < n // 2 else far_down_ref, i % (n // 2), 2, i)
        put(down_ref, i, 3, i)


def sum_y(whole, first=(), last=()):
    n = whole[0].shape[0] // Z
    feat = sum(terms[0].shape[1] for terms in (whole, first) if terms)
    out = lambda count: jax.ShapeDtypeStruct((count, feat, whole[0].shape[2]), jnp.bfloat16)
    vmem = pl.BlockSpec(memory_space=pltpu.VMEM)
    terms = [*whole, *first, *last]
    return pl.pallas_call(
        functools.partial(sum_kernel, len(whole)),
        out_shape=[out(n), out(n), out(n // 2), out(n // 2), out(n)],
        in_specs=[vmem] * len(terms),
        out_specs=[vmem] * 5,
        compiler_params=pltpu.CompilerParams(vmem_limit_bytes=16 * 2**20),
        name="sum_y",
    )(*terms)


def relays_z(mine, up, far_up, far_down, down):
    far_up, far_down = send(far_up, along_z(1)), send(far_down, along_z(-1))
    return relay_z(up, down, far_up, far_down)


def end_z(mine, relayed):
    return add(mine, send(relayed[0], along_z(1)), send(relayed[1], along_z(-1)))


def ends_y(pieces, plain, relayed):
    up, down = send(relayed[0], along_y(1)), send(relayed[1], along_y(-1))
    return [pieces[0], up, plain[1]], [pieces[1], plain[0], down]


def parts_of(count, *terms):
    n = terms[0].shape[0] // count
    return [add(*(t[d * n:(d + 1) * n] for t in terms)) for d in range(count)]


def sum_z(mine):
    return add(mine[0], *(send(mine[d], along_z(d)) for d in (1, 2, 3)))


def all_y(pieces):
    return send(pieces[1], along_y(1)), send(pieces[3], along_y(-1)), send(pieces[2], along_y(2))


def row_step(along_x, other_z, other_core):
    return [
        (r, (((r >> 2) + along_x) % X) * 4 + ((r & 3) ^ (2 * other_z) ^ other_core)) for r in range(4 * X)
    ]


def then(first, values):
    return lax.optimization_barrier((first, values))[1]


def shards(features, adjacency, tile_coords, tile_counts, weight, bias_vector):
    tiles = adjacency[0, 0]
    rows = 8 * lax.axis_size("col")
    place = tile_coords[0, 0].T
    count = tile_counts[0]
    me = lax.axis_index("col")
    y, z = me // Z, me % Z
    order = jnp.stack([
        ((y + dy) % Y) * Z + (z + dz) % Z
        for dy, dzs in ((0, range(4)), (1, range(4)), (2, (0, 1)), (2, (2, 3)), (3, range(4)))
        for dz in dzs
    ])
    kernel = lambda parts, xs, *before: partial_pieces(place, count, order, xs, tiles, rows, parts, *before)
    own = features.T
    weights = weight.reshape(lax.axis_size("row"), own.shape[0], -1)
    r = lax.axis_index("row")

    def product(hidden, steps):
        source = jnp.stack([((r // 4 + dx) % X) * 4 + ((r % 4) ^ (2 * dz) ^ core) for dx, dz, core in steps])
        w = weights[source].reshape(hidden.shape[1], -1)
        return jnp.einsum("tfm,fg->tmg", hidden, w, preferred_element_type=jnp.float32)

    get = lambda v, *step: lax.ppermute(v, "row", row_step(*step))
    swap = lambda vs: [get(v, 0, 0, 1) for v in vs]
    pair = get(own, 0, 1, 0)
    side = [get(own, 1, 0, 0), get(own, -1, 0, 0)]
    near = [own, pair]
    near += swap(near)
    pieces_a = kernel(WHOLE, near, *side)
    pair_side = [get(pair, 1, 0, 0), get(pair, -1, 0, 0)]
    swapped = swap(side)
    near_a = all_y(then(swapped, pieces_a))
    pair_side = then(pieces_a, pair_side)
    swapped += swap(pair_side)
    side, pair_side = then(swapped, (side, pair_side))
    far = [get(side[0], 1, 0, 0), get(pair_side[1], -1, 0, 0)]
    pieces_b = kernel(HALVED, side + pair_side + swapped)
    far_b = start_y(pieces_b)
    far = then((pieces_b, near_a), far)
    far_swapped = swap(far)
    plain_b = plain_y(then(far_swapped, pieces_b))
    relay_b = relay_y(pieces_b, far_b)
    pieces_c = kernel(WHOLE, far + far_swapped, *relay_b)
    near_c = all_y(pieces_c)
    mine = sum_y([pieces_a[0], *near_a], *ends_y(pieces_b, plain_b, relay_b))
    relayed = relays_z(*mine)
    hidden = end_z(mine[0], relayed)
    hidden_c = sum_z(parts_of(Z, pieces_c[0], *then(relayed, near_c)))
    on = lambda chunk: [(dx, dz, core) for core in range(2) for dx, dz in chunk]
    near = on([(0, 0), (0, 1)]) + on([(-1, 0), (1, 0), (-1, 1), (1, 1)])
    mixed = bias_vector + product(hidden, near) + product(hidden_c, on([(2, 0), (2, 1)]))
    embedded = jnp.maximum(mixed, jnp.float32(0.0)).astype(jnp.bfloat16)
    return embedded.reshape(-1, embedded.shape[-1])


def solution(mesh):
    in_specs = (
        P("col", "row"),
        P("row", "col", None, None, None),
        P("row", "col", None, None),
        P("row", "col"),
        P(),
        P(),
    )
    out_specs = P(("row", "col"), None)
    return jax.shard_map(shards, mesh=mesh, in_specs=in_specs, out_specs=out_specs, check_vma=False)
```

```python
import functools
import jax
import jax.numpy as jnp
from jax import lax
from jax.experimental import pallas as pl
from jax.experimental.pallas import tpu as pltpu
from jax.sharding import PartitionSpec as P

UNROLL = 8
WHOLE = (4, 4, 4, 4)
HALVED = (8,) * 8
SLICE = 16
LOTS = 4
VMEM_LIMIT = 44 * 2**20
X, Y, Z = 4, 4, 4


def tile_kernel(pieces, place_ref, count_ref, order_ref, *refs):
    sources, outs = refs[:-pieces - 4], refs[-pieces - 4:-4]
    total, x_ref, a_ref, sems = refs[-4:]
    *x_sources, a_source = sources[:x_ref.shape[0] // SLICE + 1]
    rows = total.shape[0] - 1
    slots, side = a_ref.shape[0], a_ref.shape[-1]
    lot = slots // LOTS
    x_copies = [
        pltpu.make_async_copy(source, x_ref.at[pl.ds(k * SLICE, SLICE)], sems.at[k])
        for k, source in enumerate(x_sources)
    ]
    a_copies = [
        pltpu.make_async_copy(
            a_source.at[pl.ds(k * lot, lot)], a_ref.at[pl.ds(k * lot, lot)], sems.at[len(x_sources) + k]
        )
        for k in range(LOTS)
    ]
    for copy in x_copies + a_copies:
        copy.start()

    def clear(i, c):
        total[i] = jnp.zeros(total.shape[1:], jnp.float32)
        return c

    lax.fori_loop(0, rows, clear, 0, unroll=4)
    count = count_ref[0]

    def add_tiles(group, c):
        products = []
        for u in range(UNROLL):
            slot = group * UNROLL + u
            row = jnp.where(slot < count, place_ref[0, slot], rows)
            nodes = pl.ds(pl.multiple_of(place_ref[1, slot] * side, side), side)
            product = lax.dot_general(
                x_ref[:, nodes], a_ref[slot], (((1,), (1,)), ((), ())), preferred_element_type=jnp.float32
            )
            products.append((row, product))
        for row, product in products:
            total[row] += product
        return c

    for copy in x_copies:
        copy.wait()
    groups = lot // UNROLL
    for k in range(LOTS):
        a_copies[k].wait()
        last = jnp.minimum(pl.cdiv(count, UNROLL), (k + 1) * groups)
        lax.fori_loop(k * groups, last, add_tiles, 0)
    per = rows // (Y * Z)
    step = 0
    for out in outs:
        for place in range(out.shape[0] // per):
            start = order_ref[step] * per
            step += 1
            for i in range(per):
                out[place * per + i] = total[start + i].astype(jnp.bfloat16)


def partial_pieces(place, count, order, xs, tiles, rows, parts, *before):
    feat, side = sum(x.shape[0] for x in xs), tiles.shape[-1]
    smem = pl.BlockSpec(memory_space=pltpu.SMEM)
    vmem = pl.BlockSpec(memory_space=pltpu.VMEM)
    hbm = pl.BlockSpec(memory_space=pltpu.HBM)
    piece = lambda part: jax.ShapeDtypeStruct((rows // part, feat, side), jnp.bfloat16)
    return pl.pallas_call(
        functools.partial(tile_kernel, len(parts)),
        out_shape=[piece(part) for part in parts],
        in_specs=[smem, smem, smem] + [hbm] * (len(xs) + 1) + [pl.BlockSpec(memory_space=pl.ANY)] * len(before),
        out_specs=[vmem] * len(parts),
        scratch_shapes=[
            pltpu.VMEM((rows + 1, feat, side), jnp.float32),
            pltpu.VMEM((feat, xs[0].shape[1]), jnp.bfloat16),
            pltpu.VMEM(tiles.shape, jnp.bfloat16),
            pltpu.SemaphoreType.DMA((len(xs) + LOTS,)),
        ],
        compiler_params=pltpu.CompilerParams(vmem_limit_bytes=VMEM_LIMIT),
        name="tile_sum",
    )(place, count, order, *xs, tiles, *before)


def along_y(step):
    return [(y * Z + z, ((y + step) % Y) * Z + z) for y in range(Y) for z in range(Z)]


def along_z(step):
    return [(y * Z + z, y * Z + (z + step) % Z) for y in range(Y) for z in range(Z)]


def add(*terms):
    out = terms[0].astype(jnp.float32)
    for term in terms[1:]:
        out = out + term.astype(jnp.float32)
    return out.astype(jnp.bfloat16)


def send(v, perm):
    return lax.ppermute(v, "col", perm)


def start_y(pieces):
    return send(pieces[4], along_y(1)), send(pieces[5], along_y(-1))


def plain_y(pieces):
    return send(pieces[3], along_y(1)), send(pieces[6], along_y(-1))


def relay_kernel(*refs):
    for near, far, out in zip(refs[:2], refs[2:4], refs[4:]):
        out[...] = (near[...].astype(jnp.float32) + far[...].astype(jnp.float32)).astype(jnp.bfloat16)


def relay_y(pieces, far):
    vmem = pl.BlockSpec(memory_space=pltpu.VMEM)
    out = jax.ShapeDtypeStruct(far[0].shape, far[0].dtype)
    return pl.pallas_call(
        relay_kernel,
        out_shape=[out, out],
        in_specs=[vmem] * 4,
        out_specs=[vmem] * 2,
        compiler_params=pltpu.CompilerParams(vmem_limit_bytes=8 * 2**20),
        name="relay_y",
    )(pieces[2], pieces[7], *far)


def relay_z(up, down, far_up, far_down):
    block = lambda index: pl.BlockSpec(far_up.shape, lambda i: (index, 0, 0))
    return pl.pallas_call(
        relay_kernel,
        grid=(1,),
        out_shape=[jax.ShapeDtypeStruct(up.shape, up.dtype)] * 2,
        in_specs=[block(0), block(1), block(0), block(0)],
        out_specs=[block(0), block(1)],
        input_output_aliases={0: 0, 1: 1},
        compiler_params=pltpu.CompilerParams(vmem_limit_bytes=8 * 2**20),
        name="relay_z",
    )(up, down, far_up, far_down)


def sum_kernel(wholes, *refs):
    whole, halved, outs = refs[:wholes], refs[wholes:-5], refs[-5:]
    mine_ref, up_ref, far_up_ref, far_down_ref, down_ref = outs
    n = mine_ref.shape[0]

    def total(refs, tile):
        out = refs[0][tile].astype(jnp.float32)
        for ref in refs[1:]:
            out = out + ref[tile].astype(jnp.float32)
        return out.astype(jnp.bfloat16)

    def put(out_ref, tile, d, i):
        few = whole[0].shape[1]
        out_ref[tile, :few] = total(whole, d * n + i)
        if halved:
            out_ref[tile, few:] = total(halved[:3] if d < 2 else halved[3:], (d % 2) * n + i)

    for i in range(n):
        put(mine_ref, i, 0, i)
        put(up_ref, i, 1, i)
        put(far_up_ref if i < n // 2 else far_down_ref, i % (n // 2), 2, i)
        put(down_ref, i, 3, i)


def sum_y(whole, first=(), last=()):
    n = whole[0].shape[0] // Z
    feat = sum(terms[0].shape[1] for terms in (whole, first) if terms)
    out = lambda count: jax.ShapeDtypeStruct((count, feat, whole[0].shape[2]), jnp.bfloat16)
    vmem = pl.BlockSpec(memory_space=pltpu.VMEM)
    terms = [*whole, *first, *last]
    return pl.pallas_call(
        functools.partial(sum_kernel, len(whole)),
        out_shape=[out(n), out(n), out(n // 2), out(n // 2), out(n)],
        in_specs=[vmem] * len(terms),
        out_specs=[vmem] * 5,
        compiler_params=pltpu.CompilerParams(vmem_limit_bytes=16 * 2**20),
        name="sum_y",
    )(*terms)


def relays_z(mine, up, far_up, far_down, down):
    far_up, far_down = send(far_up, along_z(1)), send(far_down, along_z(-1))
    return relay_z(up, down, far_up, far_down)


def end_z(mine, relayed):
    return add(mine, send(relayed[0], along_z(1)), send(relayed[1], along_z(-1)))


def ends_y(pieces, plain, relayed):
    up, down = send(relayed[0], along_y(1)), send(relayed[1], along_y(-1))
    return [pieces[0], up, plain[1]], [pieces[1], plain[0], down]


def parts_of(count, *terms):
    n = terms[0].shape[0] // count
    return [add(*(t[d * n:(d + 1) * n] for t in terms)) for d in range(count)]


def sum_z(mine):
    return [mine[0]] + [send(mine[d], along_z(d)) for d in (1, 2, 3)]


def all_y(pieces):
    return send(pieces[1], along_y(1)), send(pieces[3], along_y(-1)), send(pieces[2], along_y(2))


def row_step(along_x, other_z, other_core):
    return [
        (r, (((r >> 2) + along_x) % X) * 4 + ((r & 3) ^ (2 * other_z) ^ other_core)) for r in range(4 * X)
    ]


def then(first, values):
    return lax.optimization_barrier((first, values))[1]


def shards(features, adjacency, tile_coords, tile_counts, weight, bias_vector):
    tiles = adjacency[0, 0]
    rows = 8 * lax.axis_size("col")
    place = tile_coords[0, 0].T
    count = tile_counts[0]
    me = lax.axis_index("col")
    y, z = me // Z, me % Z
    order = jnp.stack([
        ((y + dy) % Y) * Z + (z + dz) % Z
        for dy, dzs in ((0, range(4)), (1, range(4)), (2, (0, 1)), (2, (2, 3)), (3, range(4)))
        for dz in dzs
    ])
    kernel = lambda parts, xs, *before: partial_pieces(place, count, order, xs, tiles, rows, parts, *before)
    own = features.T
    weights = weight.reshape(lax.axis_size("row"), own.shape[0], -1)
    r = lax.axis_index("row")

    def product(hidden, steps):
        source = jnp.stack([((r // 4 + dx) % X) * 4 + ((r % 4) ^ (2 * dz) ^ core) for dx, dz, core in steps])
        w = weights[source].reshape(hidden.shape[1], -1)
        return jnp.einsum("tfm,fg->tmg", hidden, w, preferred_element_type=jnp.float32)

    get = lambda v, *step: lax.ppermute(v, "row", row_step(*step))
    swap = lambda vs: [get(v, 0, 0, 1) for v in vs]
    pair = get(own, 0, 1, 0)
    side = [get(own, 1, 0, 0), get(own, -1, 0, 0)]
    near = [own, pair]
    near += swap(near)
    pieces_a = kernel(WHOLE, near, *side)
    pair_side = [get(pair, 1, 0, 0), get(pair, -1, 0, 0)]
    swapped = swap(side)
    near_a = all_y(then(swapped, pieces_a))
    pair_side = then(pieces_a, pair_side)
    swapped += swap(pair_side)
    side, pair_side = then(swapped, (side, pair_side))
    far = [get(side[0], 1, 0, 0), get(pair_side[1], -1, 0, 0)]
    pieces_b = kernel(HALVED, side + pair_side + swapped)
    far_b = start_y(pieces_b)
    far = then((pieces_b, near_a), far)
    far_swapped = swap(far)
    plain_b = plain_y(then(far_swapped, pieces_b))
    relay_b = relay_y(pieces_b, far_b)
    pieces_c = kernel(WHOLE, far + far_swapped, *relay_b)
    near_c = all_y(pieces_c)
    mine = sum_y([pieces_a[0], *near_a], *ends_y(pieces_b, plain_b, relay_b))
    relayed = relays_z(*mine)
    hidden = end_z(mine[0], relayed)
    hidden_c = sum_z(parts_of(Z, pieces_c[0], *then(relayed, near_c)))
    on = lambda chunk: [(dx, dz, core) for core in range(2) for dx, dz in chunk]
    near = on([(0, 0), (0, 1)]) + on([(-1, 0), (1, 0), (-1, 1), (1, 1)])
    mixed = bias_vector + product(hidden, near)
    mixed, hidden_c = lax.optimization_barrier((mixed, hidden_c))
    mixed = mixed + product(add(*hidden_c), on([(2, 0), (2, 1)]))
    embedded = jnp.maximum(mixed, jnp.float32(0.0)).astype(jnp.bfloat16)
    return embedded.reshape(-1, embedded.shape[-1])


def solution(mesh):
    in_specs = (
        P("col", "row"),
        P("row", "col", None, None, None),
        P("row", "col", None, None),
        P("row", "col"),
        P(),
        P(),
    )
    out_specs = P(("row", "col"), None)
    return jax.shard_map(shards, mesh=mesh, in_specs=in_specs, out_specs=out_specs, check_vma=False)
```
